256 devices in a mesh: span: 4 (over x), dom: 64 (over z, y, core).
Axes of the slice: x: 4, y: 4, z: 8, core: 2. Of those that a mesh axis runs over, the one named last changes fastest.
Arguments:
- velocity: bfloat16 [3, 256, 81, 8192], P(None, 'span', None, 'dom'), may hold values from -6 to 6
- gradient: bfloat16 [3, 256, 81, 8192], P(None, 'span', None, 'dom'), may hold values from -6 to 6
- project_table: float32 [81, 32], replicated, may hold values from -0.89 to 0.89
- jacobian: float32 [8192], P('dom'), may hold values from 0.3 to 3
- stiff_elem: float32 [32, 32, 8192], P(None, None, 'dom'), may hold values from -0.05 to 3.2, as said below
- mass_elem: float32 [32, 32, 8192], P(None, None, 'dom'), may hold values from -0.025 to 1.6, as said below
- bound_map: int32 [32, 8192], P(None, 'dom'), may hold values from 0 to 2047
Outputs:
- solution_private: float32 [256, 114688], P('span', 'dom')
- solution_interface: float32 [256, 256], P('span')
The draws below stay inside these ranges and needn't reach their ends.
Inputs may be any that keep to these rules, and one draw needn't show every extreme that they name: `bound_map`: entries below 1792 number unknowns private to the element's block of 128 elements; entries from 1792 on number the 256 interface unknowns that all blocks share. `stiff_elem`: symmetric with a dominant positive diagonal. `mass_elem`: symmetric with a dominant positive diagonal.
All inputs are finite; a program needn't handle non-finite values.
Results may differ from the reference program's by a relative error of at most 0.0003.
Values sent between devices are 32-bit elements; how exact they have to be, the bound alone decides.
A program may use at most 128 MiB of HBM per device.

```python
import math
import jax
import jax.numpy as jnp
from jax import lax

QP = 81
NBE = 32
Z = 256
ED = 128
ITERS = 3
NB = 1792
NIF = 256
ELEMS = 8192
N_DOM = 64


def element_matrix(key, width, lowest, highest):
    key_off, key_diag = jax.random.split(key)
    raw = jax.random.uniform(key_off, (NBE, NBE, ELEMS), jnp.float32, -1.0, 0.0)
    sym = 0.5 * (raw + jnp.swapaxes(raw, 0, 1)) * width
    diag = jax.random.uniform(key_diag, (NBE, ELEMS), jnp.float32, lowest, highest)
    ident = jnp.eye(NBE, dtype=jnp.float32)[:, :, None]
    return sym * (1.0 - ident) + ident * diag[None, :, :]


def table_parts(key, common_scale, own_part):
    key_common = jax.random.fold_in(key, 5)
    common = jnp.clip(jax.random.normal(key_common, (QP, 1), jnp.float32), -4.0, 4.0)
    return (common * common_scale + own_part) / 9.0


def draw_project_table(key, part):
    key = jax.random.fold_in(key, 37)
    key_own = jax.random.fold_in(key, 7)
    own_part = jnp.clip(jax.random.normal(key_own, (QP, NBE), jnp.float32), -4.0, 4.0) * 0.8
    return table_parts(key, 1.2, own_part)


def draw_stiff_elem(key, part):
    key = jax.random.fold_in(key, 11)
    return element_matrix(key, 0.05, 1.6, 3.2)


def draw_mass_elem(key, part):
    key = jax.random.fold_in(key, 23)
    return element_matrix(key, 0.025, 0.8, 1.6)


def with_ends(array, stream_key, low, largest):
    longest = array.shape.index(max(array.shape))
    spots = []
    for shift in (0, 1):
        where = [jax.random.randint(jax.random.fold_in(stream_key, axis), (), 0, length) for axis, length in enumerate(array.shape)]
        where[longest] = (where[longest] + shift) % array.shape[longest]
        spots.append(tuple(where))
    return array.at[spots[0]].set(low).at[spots[1]].set(largest)


def block_scale(stream_key, dims, cuts, smallest, top_value):
    factor_of, own = 1.0, jax.random.fold_in(stream_key, 6)
    for position, shards_of in cuts:
        draws = jnp.exp(jax.random.uniform(jax.random.fold_in(own, position), (shards_of,), jnp.float32, smallest / len(cuts), top_value / len(cuts)))
        factor_of = factor_of * jnp.repeat(draws, dims[position] // shards_of).reshape([-1 if axis == position else 1 for axis in range(len(dims))])
    return factor_of


def normal_values(own_key, shape, scale, bound, pieces=(), kind=jnp.bfloat16):
    drawn = jax.random.normal(own_key, shape, jnp.float32) * scale
    if len(pieces) > 0:
        drawn = block_scale(own_key, shape, pieces, -0.22, 0.18) * drawn
    return jnp.clip(drawn, min=-bound, max=bound).astype(kind)


def setup_inputs(seed: int = 0) -> dict:
    keys = jax.random.split(jax.random.key(seed), 8)
    return {
        "velocity": normal_values(keys[0], (3, Z, QP, ELEMS), 1.0, 6.0, ((1, 4), (3, 64))),
        "gradient": normal_values(keys[1], (3, Z, QP, ELEMS), 1.0, 6.0, ((1, 4), (3, 64))),
        "project_table": draw_project_table(jax.random.fold_in(keys[7], 71), 0),
        "jacobian": jnp.clip(jnp.exp(math.log(3.0) - 2.3025851 * jax.random.uniform(keys[3], (ELEMS,), jnp.float32) ** block_scale(keys[3], (ELEMS,), ((0, 64),), -0.2, 0.2)), 0.3, 3.0),
        "stiff_elem": draw_stiff_elem(jax.random.fold_in(keys[7], 71), 0),
        "mass_elem": draw_mass_elem(jax.random.fold_in(keys[7], 71), 0),
        "bound_map": with_ends(jax.random.randint(keys[6], (NBE, ELEMS), 0, NB + NIF), jax.random.fold_in(keys[6], 1), 0, (NB + NIF) - 1).astype(jnp.int32),
    }


time_step = 0.5
shift_base = 0.5
shift_slope = 8.0

def wave_index(index, size):
    return jnp.where(index == 1, size // 2, index // 2)

def dft_table(size):
    index = jnp.arange(size, dtype=jnp.int32)
    kappa = wave_index(index, size)
    phase = kappa[:, None] * index[None, :] % size
    angle = 2.0 * jnp.pi / size * phase.astype(jnp.float32)
    scale = jnp.where(index < 2, jnp.sqrt(1.0 / size), jnp.sqrt(2.0 / size)).astype(jnp.float32)
    odd_rows = (index % 2 == 1) & (index != 1)
    values = jnp.where(odd_rows[:, None], -jnp.sin(angle), jnp.cos(angle))
    return values * scale[:, None]

def make_forcing(velocity, gradient):
    advect = velocity[0].astype(jnp.float32) * gradient[0].astype(jnp.float32)
    advect = advect + velocity[1].astype(jnp.float32) * gradient[1].astype(jnp.float32)
    advect = advect + velocity[2].astype(jnp.float32) * gradient[2].astype(jnp.float32)
    return velocity[0].astype(jnp.float32) - time_step * advect

def reference(velocity, gradient, project_table, jacobian, stiff_elem, mass_elem, bound_map):
    high = lax.Precision.HIGHEST
    forcing = make_forcing(velocity, gradient)
    table = dft_table(Z)
    spectra = jnp.einsum('mz,zqe->mqe', table, forcing, precision=high)
    load = jnp.einsum('qb,mqe->mbe', project_table, spectra, precision=high) * jacobian
    owner = jnp.arange(ELEMS, dtype=jnp.int32) // ED
    places = jnp.where(bound_map < NB, bound_map + owner[None, :] * NB, bound_map - NB + N_DOM * NB)
    places = places.astype(jnp.int32)
    flat = places.reshape(-1)
    total = N_DOM * NB + NIF
    kappa = wave_index(jnp.arange(Z, dtype=jnp.int32), Z).astype(jnp.float32)
    shift = shift_base + shift_slope * (kappa / Z) ** 2

    def assemble(values):
        return jnp.zeros((Z, total), jnp.float32).at[:, flat].add(values.reshape(Z, -1))

    def operate(vector):
        local = vector[:, places]
        first = jnp.einsum('cbe,mbe->mce', stiff_elem, local, precision=high)
        second = jnp.einsum('cbe,mbe->mce', mass_elem, local, precision=high)
        return assemble(first + shift[:, None, None] * second)
    rhs = assemble(load)
    solution = jnp.zeros((Z, total), jnp.float32)
    residual = rhs
    direction = rhs
    norm_now = lax.optimization_barrier(jnp.sum(residual * residual, axis=1))
    for step in range(ITERS):
        image = operate(direction)
        alpha = norm_now / lax.optimization_barrier(jnp.sum(direction * image, axis=1))
        solution = solution + alpha[:, None] * direction
        residual = residual - alpha[:, None] * image
        norm_next = lax.optimization_barrier(jnp.sum(residual * residual, axis=1))
        direction = residual + (norm_next / norm_now)[:, None] * direction
        norm_now = norm_next
    return (solution[:, :N_DOM * NB], solution[:, N_DOM * NB:])
```

```python
import jax
import jax.numpy as jnp
import numpy as np
from jax import lax
from jax.experimental import pallas as pl
from jax.experimental.pallas import tpu as pltpu
from jax.sharding import PartitionSpec as P

MESH = pl.DeviceIdType.MESH
F32 = jnp.float32
BF16 = jnp.bfloat16
QP = 81
NBE = 32
ED = 128
PLANES = 64
SIZE = 256
SPAN = 4
TILES = 8
TILE = 256
PRIV = 1792
GROUP = 8
WIDE = TILE + 128
QCHUNK = 9
NT = (((1,), (1,)), ((), ()))


def spanwise_table():
    index = np.arange(SIZE)
    kappa = np.where(index == 1, SIZE // 2, index // 2)
    angle = 2.0 * np.pi / SIZE * ((kappa[:, None] * index[None, :]) % SIZE)
    scale = np.where(index < 2, np.sqrt(1.0 / SIZE), np.sqrt(2.0 / SIZE))
    odd = (index % 2 == 1) & (index != 1)
    return (np.where(odd[:, None], -np.sin(angle), np.cos(angle)) * scale[:, None]).astype(np.float32)


def split(values):
    high = values.astype(BF16)
    return high, (values - high.astype(F32)).astype(BF16)


def both(product):
    half = product.shape[0] // 2
    return product[:half] + product[half:]


def dot(left, right):
    return jnp.dot(left, right, preferred_element_type=F32)


def kernel(
    vel_hbm, grad_hbm, project, jacobian, stiff, mass, bmap, table,
    out_private, out_interface,
    vel, grad, forcing, planes, hot, parts, vparts, gathered_w, gathered_a, gathered_r,
    w8, a8, p8, r8, x8, send8, cross, modes,
    msg, recv_a, recv_b, full,
    in_sem, span_send, span_recv, dom_send, dom_recv,
):
    s = lax.axis_index("span")
    d = lax.axis_index("dom")
    zi = lax.div(d, GROUP)
    i = lax.rem(d, GROUP)

    def chunk_copies(chunk):
        rows = pl.ds(chunk * QCHUNK, QCHUNK)
        return [
            pltpu.make_async_copy(src.at[:, rows], dst.at[:, rows], in_sem.at[which, chunk])
            for which, (src, dst) in enumerate(((vel_hbm, vel), (grad_hbm, grad)))
        ]

    for chunk in range(QP // QCHUNK):
        for copy in chunk_copies(chunk):
            copy.start()

    barrier = pltpu.get_barrier_semaphore()
    for k in range(1, GROUP):
        pl.semaphore_signal(barrier, inc=1, device_id=(s, zi * GROUP + lax.rem(i + k, GROUP)), device_id_type=MESH)
        pl.semaphore_signal(barrier, inc=1, device_id=(s, lax.rem(zi + k, GROUP) * GROUP + i), device_id_type=MESH)
    for k in range(1, SPAN):
        pl.semaphore_signal(barrier, inc=1, device_id=(lax.rem(s + k, SPAN), d), device_id_type=MESH)

    @pl.loop(0, NBE)
    def _(b):
        here = bmap[pl.ds(b, 1), :]
        for g in range(0, PRIV + TILE, 256):
            rows = lax.broadcasted_iota(jnp.int32, (256, ED), 0) + g
            hot[pl.ds(g, 256), pl.ds(pl.multiple_of(b * ED, ED), ED)] = jnp.where(rows == here, 1.0, 0.0).astype(BF16)

    @pl.loop(0, QP // QCHUNK)
    def _(chunk):
        for copy in chunk_copies(chunk):
            copy.wait()

        @pl.loop(0, QCHUNK)
        def _(step):
            q = chunk * QCHUNK + step
            first = vel[0, q].astype(F32)
            advect = first * grad[0, q].astype(F32)
            advect = advect + vel[1, q].astype(F32) * grad[1, q].astype(F32)
            advect = advect + vel[2, q].astype(F32) * grad[2, q].astype(F32)
            forcing[pl.ds(pl.multiple_of(q * PLANES, PLANES), PLANES), :] = first - 0.5 * advect

    project_high, project_low = split(project[...])
    project_both = jnp.concatenate([project_high, project_low], axis=0)
    area = jnp.concatenate([jacobian[...], jacobian[...]], axis=1)

    @pl.loop(0, PLANES // 2)
    def _(pair):
        values = jnp.concatenate(
            [forcing[pl.ds(2 * pair + k, QP, stride=PLANES), :] for k in range(2)], axis=1
        )
        high, low = split(values)
        load = (both(dot(project_both, high)) + dot(project_high, low)) * area
        start = pl.multiple_of(pair * 2 * NBE, 2 * NBE)
        planes[pl.ds(start, NBE), :] = load[:, :ED]
        planes[pl.ds(start + NBE, NBE), :] = load[:, ED:]

    @pl.loop(0, NBE)
    def _(b):
        high, low = split(planes[pl.ds(b, PLANES, stride=NBE), :])
        columns = pl.ds(pl.multiple_of(b * ED, ED), ED)
        parts[:PLANES, columns] = high
        parts[PLANES:, columns] = low

    def assemble(tile):
        rows = pl.ds(pl.multiple_of(tile * TILE, TILE), TILE)
        return both(lax.dot_general(parts[...], hot[rows, :], NT, preferred_element_type=F32))

    pl.semaphore_wait(barrier, 2 * (GROUP - 1) + SPAN - 1)
    out_copies = []
    for k in (2, 1, 3, 0):
        j = lax.rem(s + k, SPAN)

        @pl.loop(0, 2)
        def _(half, j=j):
            send8[2 * j + half] = assemble(2 * j + half)

        rows = pl.ds(pl.multiple_of(s * PLANES, PLANES), PLANES)
        if k:
            copy = pltpu.make_async_remote_copy(
                src_ref=send8.at[pl.ds(2 * j, 2)], dst_ref=cross.at[:, rows],
                send_sem=span_send.at[0, k], recv_sem=span_recv.at[0, k],
                device_id=(j, d), device_id_type=MESH,
            )
            copy.start()
            out_copies.append(copy)
        else:
            cross[:, rows, :] = send8[pl.ds(2 * j, 2)]
    for copy in out_copies:
        copy.wait_recv()

    for half in range(2):
        high, low = split(cross[half])
        modes[half] = both(dot(table[...], high)) + dot(table[:SIZE, :], low)
    back_copies = []
    for k in (2, 1, 3):
        j = lax.rem(s + k, SPAN)
        copy = pltpu.make_async_remote_copy(
            src_ref=modes.at[:, pl.ds(pl.multiple_of(j * PLANES, PLANES), PLANES)], dst_ref=r8.at[pl.ds(2 * s, 2)],
            send_sem=span_send.at[1, k], recv_sem=span_recv.at[1, k],
            device_id=(j, d), device_id_type=MESH,
        )
        copy.start()
        back_copies.append(copy)
    r8[pl.ds(2 * s, 2)] = modes[:, pl.ds(pl.multiple_of(s * PLANES, PLANES), PLANES), :]
    for copy in back_copies:
        copy.wait_recv()

    def dom_sum(inst, start, width, works):
        columns = pl.ds(start, width)

        def rows_of(index):
            return pl.ds(pl.multiple_of(index * 8, 8), 8)

        def run(stage, copies):
            for copy in copies:
                copy.start()
            works[stage]()
            for copy in copies:
                copy.wait_recv()
            return copies

        def remote(stage, k, src, dst, target):
            return pltpu.make_async_remote_copy(
                src_ref=src, dst_ref=dst, send_sem=dom_send.at[inst, stage, k], recv_sem=dom_recv.at[inst, stage, k],
                device_id=(s, target), device_id_type=MESH,
            )

        copies = []
        for k in range(1, GROUP):
            peer = lax.rem(i + k, GROUP)
            copies.append(remote(0, k, msg.at[inst, rows_of(peer), columns], recv_a.at[inst, k, :, columns], zi * GROUP + peer))
        done = run(0, copies)
        total = msg[inst, rows_of(i), columns]
        for k in range(1, GROUP):
            total = total + recv_a[inst, k, :, columns]
        recv_b[inst, zi, :, columns] = total
        copies = []
        for k in range(1, GROUP):
            peer = lax.rem(zi + k, GROUP)
            own = recv_b.at[inst, zi, :, columns]
            copies.append(remote(1, k, own, own, peer * GROUP + i))
        done = done + run(1, copies)
        total = recv_b[inst, 0, :, columns]
        for k in range(1, GROUP):
            total = total + recv_b[inst, k, :, columns]
        full[inst, rows_of(i), columns] = total
        copies = []
        for k in range(1, GROUP):
            own = full.at[inst, rows_of(i), columns]
            copies.append(remote(2, k, own, own, zi * GROUP + lax.rem(i + k, GROUP)))
        done = done + run(2, copies)
        for copy in done:
            copy.wait_send()

    def keep_parts(tile, values):
        high, low = split(values)
        columns = pl.ds(pl.multiple_of(tile * TILE, TILE), TILE)
        vparts[:PLANES, columns] = high
        vparts[PLANES:, columns] = low

    def gather_private(first, last):
        @pl.loop(first, last)
        def _(n):
            columns = pl.ds(pl.multiple_of(n * TILE, TILE), TILE)
            out = both(dot(vparts[:, :PRIV], hot[:PRIV, columns]))
            gathered_w[2 * n] = out[:, :ED]
            gathered_w[2 * n + 1] = out[:, ED:]

    def gather_interface(values):
        keep_parts(TILES - 1, values)
        lhs = vparts[:, PRIV:]

        @pl.loop(0, NBE // 2)
        def _(n):
            columns = pl.ds(pl.multiple_of(n * TILE, TILE), TILE)
            out = both(dot(lhs, hot[PRIV:, columns]))
            gathered_w[2 * n] += out[:, :ED]
            gathered_w[2 * n + 1] += out[:, ED:]

    def assemble_private(first, last):
        @pl.loop(first, last)
        def _(tile):
            values = assemble(tile)
            w8[tile] = values
            keep_parts(tile, values)

    def nothing():
        pass

    lane = lax.broadcasted_iota(jnp.int32, (PLANES, 128), 1)
    mode = lax.broadcasted_iota(jnp.int32, (PLANES, 128), 0) + s * PLANES
    kappa = jnp.where(mode == 1, SIZE // 2, lax.shift_right_logical(mode, 1)).astype(F32) * (1.0 / SIZE)
    shift = 0.5 + 8.0 * kappa * kappa

    def operate(source):
        def column(c, products):
            first = jnp.zeros((PLANES, ED), F32)
            second = jnp.zeros((PLANES, ED), F32)
            for b in range(NBE):
                values = source[b]
                first = first + stiff[c, pl.ds(b, 1), :] * values
                second = second + mass[c, pl.ds(b, 1), :] * values
            image = first + shift * second
            high, low = split(image)
            columns = pl.ds(pl.multiple_of(c * ED, ED), ED)
            parts[:PLANES, columns] = high
            parts[PLANES:, columns] = low
            return products + image * source[c]

        return jnp.sum(lax.fori_loop(0, NBE, column, jnp.zeros((PLANES, ED), F32)), axis=1, keepdims=True)

    def square_sum(left, right):
        total = jnp.zeros((PLANES, 1), F32)
        for t in range(TILES - 1):
            total = total + jnp.sum(left[t] * right[t], axis=1, keepdims=True)
        return total

    def put_dots(inst, rr, rw, ra):
        msg[inst, :, TILE:] = jnp.where(lane == 0, rr, jnp.where(lane == 1, rw, jnp.where(lane == 2, ra, 0.0)))

    msg[0, :, :TILE] = r8[TILES - 1]
    for t in range(TILES - 1):
        keep_parts(t, r8[t])
    dom_sum(0, 0, TILE, [lambda: gather_private(0, 5), lambda: gather_private(5, 10), lambda: gather_private(10, 16)])
    r_int = full[0, :, :TILE]
    r8[TILES - 1] = r_int
    gather_interface(r_int)

    gathered_r[...] = gathered_w[...]
    works = [
        lambda: assemble_private(0, 4),
        lambda: (assemble_private(4, 7), gather_private(0, 2)),
        lambda: gather_private(2, 16),
    ]

    norm = None
    energy = None
    alpha = None
    for step in range(3):
        inst = step + 1
        rw = operate(gathered_r)
        rr = square_sum(r8, r8)
        ra = square_sum(r8, a8) if step else jnp.zeros_like(rr)
        put_dots(inst, rr, rw, ra)
        if step < 2:
            msg[inst, :, :TILE] = assemble(TILES - 1)
            dom_sum(inst, 0, WIDE, works)
        else:
            dom_sum(inst, TILE, 128, [nothing] * 3)
        dots = full[inst, :, TILE:]
        r_int = r8[TILES - 1]
        rr = dots[:, 0:1] + jnp.sum(r_int * r_int, axis=1, keepdims=True)
        rw = dots[:, 1:2]
        if step:
            ra = dots[:, 2:3] + jnp.sum(r_int * a8[TILES - 1], axis=1, keepdims=True)
            beta = rr / norm
            energy = rw + 2.0 * beta * ra + beta * beta * energy
        else:
            energy = rw
        norm = rr
        alpha = norm / energy
        if step < 2:
            w_int = full[inst, :, :TILE]
            w8[TILES - 1] = w_int
            gather_interface(w_int)

            @pl.loop(0, NBE)
            def _(b):
                image = gathered_w[b]
                if step:
                    image = image + beta * gathered_a[b]
                if step < 1:
                    gathered_a[b] = image
                gathered_r[b] = gathered_r[b] - alpha * image

        for t in range(TILES):
            direction = r8[t]
            if step:
                direction = direction + beta * p8[t]
                iterate = x8[t] + alpha * direction
            else:
                iterate = alpha * direction
            if step < 2:
                p8[t] = direction
                x8[t] = iterate
                image = w8[t]
                if step:
                    image = image + beta * a8[t]
                a8[t] = image
                r8[t] = r8[t] - alpha * image
            elif t < TILES - 1:
                out_private[:, t * TILE:(t + 1) * TILE] = iterate
            else:
                out_interface[...] = iterate

    for copy in out_copies + back_copies:
        copy.wait_send()


def shards(velocity, gradient, project_table, jacobian, stiff_elem, mass_elem, bound_map):
    table = spanwise_table()
    high = table.astype(BF16)
    low = (table - high.astype(np.float32)).astype(BF16)
    vmem = pl.BlockSpec(memory_space=pltpu.VMEM)
    hbm = pl.BlockSpec(memory_space=pl.ANY)
    field = pltpu.VMEM((TILES, PLANES, TILE), F32)
    spread = pltpu.VMEM((NBE, PLANES, ED), F32)
    return pl.pallas_call(
        kernel,
        out_shape=(
            jax.ShapeDtypeStruct((PLANES, PRIV), F32),
            jax.ShapeDtypeStruct((PLANES, TILE), F32),
        ),
        in_specs=[hbm, hbm] + [vmem] * 6,
        out_specs=(vmem, vmem),
        scratch_shapes=[
            pltpu.VMEM((3, QP, PLANES, ED), BF16),
            pltpu.VMEM((3, QP, PLANES, ED), BF16),
            pltpu.VMEM((QP * PLANES, ED), F32),
            pltpu.VMEM((PLANES * NBE, ED), F32),
            pltpu.VMEM((TILES * TILE, NBE * ED), BF16),
            pltpu.VMEM((2 * PLANES, NBE * ED), BF16),
            pltpu.VMEM((2 * PLANES, TILES * TILE), BF16),
            spread, spread, spread,
            field, field, field, field, field, field,
            pltpu.VMEM((2, SIZE, TILE), F32),
            pltpu.VMEM((2, SIZE, TILE), F32),
            pltpu.VMEM((4, PLANES, WIDE), F32),
            pltpu.VMEM((4, GROUP, 8, WIDE), F32),
            pltpu.VMEM((4, GROUP, 8, WIDE), F32),
            pltpu.VMEM((4, PLANES, WIDE), F32),
            pltpu.SemaphoreType.DMA((2, QP // QCHUNK)),
            pltpu.SemaphoreType.DMA((2, SPAN)),
            pltpu.SemaphoreType.DMA((2, SPAN)),
            pltpu.SemaphoreType.DMA((4, 3, GROUP)),
            pltpu.SemaphoreType.DMA((4, 3, GROUP)),
        ],
        compiler_params=pltpu.CompilerParams(
            collective_id=0, has_side_effects=True, vmem_limit_bytes=56 * 1024 * 1024
        ),
    )(
        jnp.transpose(velocity, (0, 2, 1, 3)),
        jnp.transpose(gradient, (0, 2, 1, 3)),
        project_table.T,
        jacobian.reshape(1, ED),
        stiff_elem,
        mass_elem,
        bound_map,
        jnp.concatenate([jnp.asarray(high), jnp.asarray(low)], axis=0),
    )


def solution(mesh):
    return jax.shard_map(
        shards,
        mesh=mesh,
        in_specs=(
            P(None, "span", None, "dom"),
            P(None, "span", None, "dom"),
            P(),
            P("dom"),
            P(None, None, "dom"),
            P(None, None, "dom"),
            P(None, "dom"),
        ),
        out_specs=(P("span", "dom"), P("span", None)),
        check_vma=False,
    )
```

```python
import jax
import jax.numpy as jnp
import numpy as np
from jax import lax
from jax.experimental import pallas as pl
from jax.experimental.pallas import tpu as pltpu
from jax.sharding import PartitionSpec as P

MESH = pl.DeviceIdType.MESH
F32 = jnp.float32
BF16 = jnp.bfloat16
QP = 81
NBE = 32
ED = 128
PLANES = 64
SIZE = 256
SPAN = 4
TILES = 8
TILE = 256
PRIV = 1792
GROUP = 8
WIDE = TILE + 128


def spanwise_table():
    index = np.arange(SIZE)
    kappa = np.where(index == 1, SIZE // 2, index // 2)
    angle = 2.0 * np.pi / SIZE * ((kappa[:, None] * index[None, :]) % SIZE)
    scale = np.where(index < 2, np.sqrt(1.0 / SIZE), np.sqrt(2.0 / SIZE))
    odd = (index % 2 == 1) & (index != 1)
    return (np.where(odd[:, None], -np.sin(angle), np.cos(angle)) * scale[:, None]).astype(np.float32)


def split(values):
    high = values.astype(BF16)
    return high, (values - high.astype(F32)).astype(BF16)


def both(product):
    half = product.shape[0] // 2
    return product[:half] + product[half:]


def dot(left, right):
    return jnp.dot(left, right, preferred_element_type=F32)


def kernel(
    vel_hbm, grad_hbm, project, jacobian, bmap, stiff_hbm, mass_hbm, table_hbm, wrap_hbm,
    out,
    stiff, mass, table, wrap, cols, rows_hot, shifted, parts, vparts, gathered_w, gathered_a, gathered_r,
    w8, a8, p8, r8, x8, cross, modes, interface,
    msg, recv_a, recv_b, full, dots_a, dots_b, factors, state,
    in_sem, span_send, span_recv, dom_send, dom_recv,
):
    s = lax.axis_index("span")
    d = lax.axis_index("dom")
    zi = lax.div(d, GROUP)
    i = lax.rem(d, GROUP)

    chunks = [(0, 32), (32, 32), (64, QP - 64)]

    def chunk_copies(index):
        start, count = chunks[index]
        copies = []
        for which, source in enumerate((vel_hbm, grad_hbm)):
            for c in range(3):
                slab = which * 9 + c * 3 + index
                copies.append(pltpu.make_async_copy(
                    source.at[c, pl.ds(start * PLANES, count * PLANES)],
                    cols.at[slab, pl.ds(0, count * PLANES)],
                    in_sem.at[slab],
                ))
        return copies

    for index in range(3):
        for copy in chunk_copies(index):
            copy.start()

    small_copies = [
        pltpu.make_async_copy(src, dst, in_sem.at[18 + k])
        for k, (src, dst) in enumerate(((stiff_hbm, stiff), (mass_hbm, mass), (table_hbm, table), (wrap_hbm, wrap)))
    ]
    for copy in small_copies:
        copy.start()

    barrier = pltpu.get_barrier_semaphore()
    def start(copies):
        first, last, make = copies

        @pl.loop(first, last)
        def _(k):
            make(k).start()

        return copies

    def arrive(copies):
        first, last, make = copies

        @pl.loop(first, last)
        def _(k):
            make(k).wait_recv()

    def leave(*groups):
        for first, last, make in groups:
            @pl.loop(first, last)
            def _(k, make=make):
                make(k).wait_send()

    def same_z(k):
        return zi * GROUP + lax.rem(i + k, GROUP)

    def along_z(k):
        return lax.rem(zi + k, GROUP) * GROUP + i

    @pl.loop(1, GROUP)
    def _(k):
        pl.semaphore_signal(barrier, inc=1, device_id=(s, same_z(k)), device_id_type=MESH)
        pl.semaphore_signal(barrier, inc=1, device_id=(s, along_z(k)), device_id_type=MESH)

    @pl.loop(1, SPAN)
    def _(k):
        pl.semaphore_signal(barrier, inc=1, device_id=(lax.rem(s + k, SPAN), d), device_id_type=MESH)

    @pl.loop(0, NBE, unroll=2)
    def _(b):
        here = jnp.transpose(jnp.broadcast_to(bmap[pl.ds(b, 1), :], (ED, ED)))
        lane = lax.broadcasted_iota(jnp.int32, (16, ED), 1)
        for r in range(0, ED, 16):
            tile = lax.shift_right_logical(here[r:r + 16], 7).astype(F32).astype(BF16)
            hot = jnp.where((here[r:r + 16] & (ED - 1)) == lane, 1.0, 0.0).astype(BF16)
            for j in range(TILES * TILE // ED):
                rows_hot[pl.ds(pl.multiple_of(b * ED + r, 16), 16), j * ED:(j + 1) * ED] = jnp.where(
                    tile == jnp.bfloat16(j), hot, jnp.zeros_like(hot)
                )

    for index in range(3):
        for copy in chunk_copies(index):
            copy.wait()

        @pl.loop(0, chunks[index][1])
        def _(q, index=index):
            here = pl.ds(pl.multiple_of(q * PLANES, PLANES), PLANES)

            def value(which, c):
                return cols[which * 9 + c * 3 + index, here].astype(F32)

            first = value(0, 0)
            advect = first * value(1, 0) + value(0, 1) * value(1, 1) + value(0, 2) * value(1, 2)
            row = pl.multiple_of((q + chunks[index][0]) * PLANES, PLANES)
            shifted[pl.ds(row, PLANES), :] = first - 0.5 * advect

    project_high, project_low = split(project[...])
    project_both = jnp.concatenate([project_high, project_low], axis=0)
    area = jnp.concatenate([jacobian[...], jacobian[...]], axis=1)
    loads = QP * PLANES

    @pl.loop(0, PLANES // 2, unroll=4)
    def _(pair):
        values = jnp.concatenate(
            [shifted[pl.ds(2 * pair + k, QP, stride=PLANES), :] for k in range(2)], axis=1
        )
        high, low = split(values)
        load = (both(dot(project_both, high)) + dot(project_high, low)) * area
        start = pl.multiple_of(loads + pair * 2 * NBE, 2 * NBE)
        shifted[pl.ds(start, NBE), :] = load[:, :ED]
        shifted[pl.ds(start + NBE, NBE), :] = load[:, ED:]

    @pl.loop(0, NBE, unroll=4)
    def _(b):
        high, low = split(shifted[pl.ds(loads + b, PLANES, stride=NBE), :])
        columns = pl.ds(pl.multiple_of(b * ED, ED), ED)
        parts[:PLANES, columns] = high
        parts[PLANES:, columns] = low

    def remote(inst, stage, k, src, dst, target):
        return pltpu.make_async_remote_copy(
            src_ref=src, dst_ref=dst, send_sem=dom_send.at[inst, stage, k], recv_sem=dom_recv.at[inst, stage, k],
            device_id=(s, target), device_id_type=MESH,
        )

    def across(stage, k, src, dst):
        return pltpu.make_async_remote_copy(
            src_ref=src, dst_ref=dst, send_sem=span_send.at[stage, k], recv_sem=span_recv.at[stage, k],
            device_id=(lax.rem(s + k, SPAN), d), device_id_type=MESH,
        )

    def rows_of(index):
        return pl.ds(pl.multiple_of(index * 8, 8), 8)

    def scatter_sum(inst, columns):
        def make(k):
            peer = lax.rem(i + k, GROUP)
            return remote(
                inst, 0, k, msg.at[inst, rows_of(peer), columns], recv_a.at[inst, k, :, columns], zi * GROUP + peer
            )

        return start((1, GROUP, make))

    def depth_sum(inst, columns):
        total = msg[inst, rows_of(i), columns]
        for k in range(1, GROUP):
            total = total + recv_a[inst, k, :, columns]
        recv_b[inst, zi, :, columns] = total
        own = recv_b.at[inst, zi, :, columns]
        return start((1, GROUP, lambda k: remote(inst, 1, k, own, own, along_z(k))))

    def depth_total(inst, columns):
        total = recv_b[inst, 0, :, columns]
        for k in range(1, GROUP):
            total = total + recv_b[inst, k, :, columns]
        return total

    def within(inst, stage, own):
        return start((1, GROUP, lambda k: remote(inst, stage, k, own, own, same_z(k))))

    def assemble(first, count):
        return both(dot(parts[...], rows_hot[:, first * TILE:(first + count) * TILE]))

    shared = pl.ds(0, TILE)
    msg[0, :, shared] = assemble(TILES - 1, 1)
    pl.semaphore_wait(barrier, 2 * (GROUP - 1) + SPAN - 1)
    int_a = scatter_sum(0, shared)
    rows = pl.ds(pl.multiple_of(s * PLANES, PLANES), PLANES)

    def out_copy(k):
        return across(0, k, w8.at[pl.ds(2 * lax.rem(s + k, SPAN), 2)], cross.at[:, rows])

    @pl.loop(1, SPAN + 1)
    def _(k):
        j = lax.rem(s + k, SPAN)
        chunk = both(dot(parts[...], rows_hot[:, pl.ds(pl.multiple_of(j * 2 * TILE, 2 * TILE), 2 * TILE)]))
        for half in range(2):
            w8[2 * j + half] = chunk[:, half * TILE:(half + 1) * TILE]

        @pl.when(k < SPAN)
        def _():
            out_copy(k).start()

    out_copies = (1, SPAN, out_copy)
    cross[:, rows, :] = w8[pl.ds(2 * s, 2)]
    arrive(int_a)
    int_b = depth_sum(0, shared)

    for copy in small_copies:
        copy.wait()
    wave = (lax.broadcasted_iota(jnp.int32, (PLANES // 2, ED), 0) + s * (PLANES // 2)).astype(F32) * (1.0 / SIZE)
    shift = 0.5 + 8.0 * wave * wave

    @pl.loop(0, NBE)
    def _(c):
        for b in range(NBE):
            row = pl.multiple_of((c * NBE + b) * (PLANES // 2), PLANES // 2)
            shifted[pl.ds(row, PLANES // 2), :] = stiff[c, pl.ds(b, 1), :] + shift * mass[c, pl.ds(b, 1), :]

    arrive(out_copies)

    @pl.loop(0, 2)
    def _(half):
        high, low = split(cross[half])
        modes[half] = both(dot(table[...], high)) + dot(table[:SIZE, :], low)

    def back_copy(k):
        there = pl.ds(pl.multiple_of(lax.rem(s + k, SPAN) * PLANES, PLANES), PLANES)
        return across(1, k, modes.at[:, there], r8.at[pl.ds(2 * s, 2)])

    back_copies = start((1, SPAN, back_copy))
    r8[pl.ds(2 * s, 2)] = modes[:, pl.ds(pl.multiple_of(s * PLANES, PLANES), PLANES), :]

    arrive(int_b)
    interface[i, s] = depth_total(0, shared)
    int_c = start((1, SPAN, lambda k: across(2, k, interface.at[i, s], interface.at[i, s])))

    @pl.loop(0, NBE)
    def _(b):
        here = jnp.broadcast_to(bmap[pl.ds(b, 1), :], (16, ED))
        row = lax.broadcasted_iota(jnp.int32, (16, ED), 0)
        tile = lax.shift_right_logical(here, 4).astype(F32).astype(BF16)
        hot = jnp.where((here & 15) == row, 1.0, 0.0).astype(BF16)
        for g in range(TILES * TILE // 16):
            cols[b, pl.ds(g * 16, 16), :] = jnp.where(tile == jnp.bfloat16(g), hot, jnp.zeros_like(hot))

    arrive(int_c)
    int_d = within(0, 2, interface.at[i])
    for field in (a8, p8, x8, gathered_a):
        field[...] = jnp.zeros_like(field)

    def keep_parts(tile, values):
        high, low = split(values)
        columns = pl.ds(pl.multiple_of(tile * TILE, TILE), TILE)
        vparts[:PLANES, columns] = high
        vparts[PLANES:, columns] = low

    def gather_private(target):
        @pl.loop(0, 4)
        def _(n):
            hot = jnp.concatenate([cols[n * 8 + k, :PRIV] for k in range(8)], axis=1)
            out = both(dot(vparts[:, :PRIV], hot))
            for k in range(8):
                target[8 * n + k] = out[:, k * ED:(k + 1) * ED]

    def gather_interface(target, values):
        high, low = split(values)
        rest = (values - high.astype(F32) - low.astype(F32)).astype(BF16)
        lhs = jnp.concatenate([high, low, rest], axis=0)
        for n in range(4):
            hot = jnp.concatenate([cols[n * 8 + k, PRIV:] for k in range(8)], axis=1)
            out = dot(lhs, hot)
            out = out[:PLANES] + out[PLANES:2 * PLANES] + out[2 * PLANES:]
            for k in range(8):
                target[8 * n + k] += out[:, k * ED:(k + 1) * ED]

    leave(out_copies)
    arrive(back_copies)

    @pl.loop(0, TILES - 1)
    def _(t):
        keep_parts(t, r8[t])

    gather_private(gathered_r)
    arrive(int_d)
    high, low = split(interface[...].reshape(SIZE, TILE))
    wrap_high = wrap[pl.ds(pl.multiple_of(s * PLANES, PLANES), PLANES), :]
    wrap_low = wrap[pl.ds(pl.multiple_of(SIZE + s * PLANES, PLANES), PLANES), :]
    r_int = dot(wrap_high, high) + dot(wrap_low, high) + dot(wrap_high, low)
    r8[TILES - 1] = r_int
    gather_interface(gathered_r, r_int)
    leave(int_a, int_b, int_c, int_d, back_copies)

    def dom_sum(inst):
        columns = pl.ds(0, WIDE)
        first = scatter_sum(inst, columns)
        assemble_private()
        arrive(first)
        second = depth_sum(inst, columns)
        gather_private(gathered_w)
        arrive(second)
        full[inst, rows_of(i), columns] = depth_total(inst, columns)
        third = within(inst, 2, full.at[inst, rows_of(i), columns])
        arrive(third)
        leave(first, second, third)

    def dots_sum(values):
        square = jnp.concatenate([values, jnp.zeros_like(values)], axis=0)
        dots_a[i] = jnp.transpose(square)[:8]
        first = within(0, 3, dots_a.at[i])
        arrive(first)
        total = dots_a[0]
        for k in range(1, GROUP):
            total = total + dots_a[k]
        dots_b[zi] = total
        own = dots_b.at[zi]
        second = start((1, GROUP, lambda k: remote(1, 3, k, own, own, along_z(k))))
        arrive(second)
        total = dots_b[0]
        for k in range(1, GROUP):
            total = total + dots_b[k]
        leave(first, second)
        square = jnp.concatenate([total, jnp.zeros((ED - 8, ED), F32)], axis=0)
        return jnp.transpose(square)[:PLANES]

    def assemble_private():
        @pl.loop(0, TILES // 2)
        def _(pair):
            columns = pl.ds(pl.multiple_of(pair * 2 * TILE, 2 * TILE), 2 * TILE)
            out = both(dot(parts[...], rows_hot[:, columns]))
            for half in range(2):
                values = out[:, half * TILE:(half + 1) * TILE]
                w8[2 * pair + half] = values
                keep_parts(2 * pair + half, values)

    lane = lax.broadcasted_iota(jnp.int32, (PLANES, ED), 1)
    extra = jnp.where(s == 0, 2.0, 0.0)
    top = lax.broadcasted_iota(jnp.int32, (PLANES // 2, ED), 0) == 0
    half_rows = PLANES // 2
    block = 4

    def operate(source):
        special = source[:, half_rows, :] * extra

        @pl.loop(0, NBE // block)
        def _(step):
            sums = [[jnp.zeros((half_rows, ED), F32) for _ in range(2)] for _ in range(block)]
            for b in range(NBE):
                even = source[b, :half_rows]
                odd = source[b, half_rows:]
                for k in range(block):
                    row = pl.multiple_of(((step * block + k) * NBE + b) * half_rows, half_rows)
                    matrix = shifted[pl.ds(row, half_rows), :]
                    sums[k][0] = sums[k][0] + matrix * even
                    sums[k][1] = sums[k][1] + matrix * odd
            for k in range(block):
                gathered_w[step * block + k, :half_rows] = sums[k][0]
                gathered_w[step * block + k, half_rows:] = sums[k][1]

        def column(c, products):
            fix = jnp.sum(mass[c] * special, axis=0, keepdims=True)
            image = jnp.concatenate(
                [gathered_w[c, :half_rows], gathered_w[c, half_rows:] + jnp.where(top, fix, 0.0)], axis=0
            )
            high, low = split(image)
            columns = pl.ds(pl.multiple_of(c * ED, ED), ED)
            parts[:PLANES, columns] = high
            parts[PLANES:, columns] = low
            return products + image * source[c]

        products = lax.fori_loop(0, NBE, column, jnp.zeros((PLANES, ED), F32), unroll=4)
        return jnp.sum(products, axis=1, keepdims=True)

    def product_sum(left, right):
        total = left[0] * right[0]
        for t in range(1, TILES - 1):
            total = total + left[t] * right[t]
        return jnp.sum(total, axis=1, keepdims=True)

    state[0] = jnp.ones((PLANES, ED), F32)
    state[1] = jnp.zeros((PLANES, ED), F32)

    @pl.loop(0, 3)
    def _(step):
        rw = operate(gathered_r)
        rr = product_sum(r8, r8)
        ra = product_sum(r8, a8)
        own = jnp.where(lane == 0, rr, jnp.where(lane == 1, rw, jnp.where(lane == 2, ra, 0.0)))

        @pl.when(step < 2)
        def _():
            msg[step + 1, :, :TILE] = assemble(TILES - 1, 1)
            msg[step + 1, :, TILE:] = own
            dom_sum(step + 1)
            state[2] = full[step + 1, :, TILE:]

        @pl.when(step == 2)
        def _():
            state[2] = dots_sum(own)

        r_int = r8[TILES - 1]
        rr = state[2, :, 0:1] + jnp.sum(r_int * r_int, axis=1, keepdims=True)
        rw = state[2, :, 1:2]
        ra = state[2, :, 2:3] + jnp.sum(r_int * a8[TILES - 1], axis=1, keepdims=True)
        beta = jnp.where(step == 0, 0.0, rr / state[0, :, 0:1])
        energy = rw + 2.0 * beta * ra + beta * beta * state[1, :, 0:1]
        state[0] = jnp.broadcast_to(rr, (PLANES, ED))
        state[1] = jnp.broadcast_to(energy, (PLANES, ED))
        factors[0] = jnp.broadcast_to(rr / energy, (PLANES, TILE))
        factors[1] = jnp.broadcast_to(beta, (PLANES, TILE))

        @pl.when(step < 2)
        def _():
            w_int = full[step + 1, :, :TILE]
            w8[TILES - 1] = w_int
            gather_interface(gathered_w, w_int)

            @pl.loop(0, NBE, unroll=2)
            def _(b):
                image = gathered_w[b] + factors[1, :, :ED] * gathered_a[b]
                gathered_a[b] = image
                gathered_r[b] = gathered_r[b] - factors[0, :, :ED] * image

        @pl.loop(0, TILES)
        def _(t):
            direction = r8[t] + factors[1] * p8[t]
            p8[t] = direction
            x8[t] = x8[t] + factors[0] * direction
            image = w8[t] + factors[1] * a8[t]
            a8[t] = image
            r8[t] = r8[t] - factors[0] * image

    @pl.loop(0, TILES)
    def _(t):
        for part in range(2):
            slab = out.at[2 * t + part]
            for parity in range(2):
                mine = x8[t, parity * half_rows:(parity + 1) * half_rows, part * ED:(part + 1) * ED]
                slab[pl.ds(parity, half_rows, stride=2), :] = mine


def place(slabs, out_private, out_interface):
    for n in range(TILES * TILE // ED):
        if n < PRIV // ED:
            out_private[:, n * ED:(n + 1) * ED] = slabs[n]
        else:
            out_interface[:, n * ED - PRIV:(n + 1) * ED - PRIV] = slabs[n]


def shards(velocity, gradient, project_table, jacobian, stiff_elem, mass_elem, bound_map):
    order = np.arange(SIZE).reshape(SPAN, PLANES // 2, 2).transpose(0, 2, 1).reshape(-1)
    table = spanwise_table()[order]
    wrap = table[:, np.arange(SIZE).reshape(SPAN, GROUP, 8).transpose(1, 0, 2).reshape(-1)]

    def in_parts(values):
        high = values.astype(BF16)
        return jnp.asarray(np.concatenate([high, (values - high.astype(np.float32)).astype(BF16)], axis=0))

    vmem = pl.BlockSpec(memory_space=pltpu.VMEM)
    hbm = pl.BlockSpec(memory_space=pl.ANY)
    field = pltpu.VMEM((TILES, PLANES, TILE), F32)
    spread = pltpu.VMEM((NBE, PLANES, ED), F32)
    slabs = pl.pallas_call(
        kernel,
        out_shape=jax.ShapeDtypeStruct((TILES * TILE // ED, PLANES, ED), F32),
        in_specs=[hbm, hbm] + [vmem] * 3 + [hbm] * 4,
        out_specs=vmem,
        scratch_shapes=[
            pltpu.VMEM((NBE, NBE, ED), F32),
            pltpu.VMEM((NBE, NBE, ED), F32),
            pltpu.VMEM((2 * SIZE, SIZE), BF16),
            pltpu.VMEM((2 * SIZE, SIZE), BF16),
            pltpu.VMEM((NBE, TILES * TILE, ED), BF16),
            pltpu.VMEM((NBE * ED, TILES * TILE), BF16),
            pltpu.VMEM((NBE * NBE * PLANES // 2, ED), F32),
            pltpu.VMEM((2 * PLANES, NBE * ED), BF16),
            pltpu.VMEM((2 * PLANES, TILES * TILE), BF16),
            spread, spread, spread,
            field, field, field, field, field,
            pltpu.VMEM((2, SIZE, TILE), F32),
            pltpu.VMEM((2, SIZE, TILE), F32),
            pltpu.VMEM((GROUP, SPAN, 8, TILE), F32),
            pltpu.VMEM((3, PLANES, WIDE), F32),
            pltpu.VMEM((3, GROUP, 8, WIDE), F32),
            pltpu.VMEM((3, GROUP, 8, WIDE), F32),
            pltpu.VMEM((3, PLANES, WIDE), F32),
            pltpu.VMEM((GROUP, 8, ED), F32),
            pltpu.VMEM((GROUP, 8, ED), F32),
            pltpu.VMEM((2, PLANES, TILE), F32),
            pltpu.VMEM((3, PLANES, ED), F32),
            pltpu.SemaphoreType.DMA((22,)),
            pltpu.SemaphoreType.DMA((3, SPAN)),
            pltpu.SemaphoreType.DMA((3, SPAN)),
            pltpu.SemaphoreType.DMA((3, 4, GROUP)),
            pltpu.SemaphoreType.DMA((3, 4, GROUP)),
        ],
        compiler_params=pltpu.CompilerParams(
            collective_id=0, has_side_effects=True, vmem_limit_bytes=62 * 1024 * 1024
        ),
    )(
        jnp.transpose(velocity, (0, 2, 1, 3)).reshape(3, QP * PLANES, ED),
        jnp.transpose(gradient, (0, 2, 1, 3)).reshape(3, QP * PLANES, ED),
        project_table.T,
        jacobian.reshape(1, ED),
        bound_map,
        stiff_elem,
        mass_elem,
        in_parts(table),
        in_parts(wrap),
    )
    return pl.pallas_call(
        place,
        out_shape=(jax.ShapeDtypeStruct((PLANES, PRIV), F32), jax.ShapeDtypeStruct((PLANES, TILE), F32)),
        in_specs=[vmem],
        out_specs=(vmem, vmem),
    )(slabs)


def solution(mesh):
    return jax.shard_map(
        shards,
        mesh=mesh,
        in_specs=(
            P(None, "span", None, "dom"),
            P(None, "span", None, "dom"),
            P(),
            P("dom"),
            P(None, None, "dom"),
            P(None, None, "dom"),
            P(None, "dom"),
        ),
        out_specs=(P("span", "dom"), P("span", None)),
        check_vma=False,
    )
```

```python
import jax
import jax.numpy as jnp
import numpy as np
from jax import lax
from jax.experimental import pallas as pl
from jax.experimental.pallas import tpu as pltpu
from jax.sharding import PartitionSpec as P

MESH = pl.DeviceIdType.MESH
F32 = jnp.float32
BF16 = jnp.bfloat16
QP = 81
NBE = 32
ED = 128
PLANES = 64
SIZE = 256
SPAN = 4
TILES = 8
TILE = 256
PRIV = 1792
GROUP = 8


def spanwise_table():
    index = np.arange(SIZE)
    kappa = np.where(index == 1, SIZE // 2, index // 2)
    angle = 2.0 * np.pi / SIZE * ((kappa[:, None] * index[None, :]) % SIZE)
    scale = np.where(index < 2, np.sqrt(1.0 / SIZE), np.sqrt(2.0 / SIZE))
    odd = (index % 2 == 1) & (index != 1)
    return (np.where(odd[:, None], -np.sin(angle), np.cos(angle)) * scale[:, None]).astype(np.float32)


def split(values):
    high = values.astype(BF16)
    return high, (values - high.astype(F32)).astype(BF16)


def both(product):
    half = product.shape[0] // 2
    return product[:half] + product[half:]


def dot(left, right):
    return jnp.dot(left, right, preferred_element_type=F32)


def kernel(
    vel_hbm, grad_hbm, project, jacobian, bmap, stiff_hbm, mass_hbm, table_hbm, wrap_hbm,
    out,
    stiff, mass, table, wrap, cols, rows_hot, shifted, parts, vparts, gathered_w, gathered_a, gathered_r,
    w8, a8, p8, r8, x8, cross, modes, interface,
    msg, recv_a, recv_b, full, dots_a, dots_b, factors, state,
    in_sem, span_send, span_recv, dom_send, dom_recv,
):
    s = lax.axis_index("span")
    d = lax.axis_index("dom")
    zi = lax.div(d, GROUP)
    i = lax.rem(d, GROUP)

    chunks = [(0, 32), (32, 32), (64, QP - 64)]

    def chunk_copies(index):
        start, count = chunks[index]
        copies = []
        for which, source in enumerate((vel_hbm, grad_hbm)):
            for c in range(3):
                slab = which * 9 + c * 3 + index
                copies.append(pltpu.make_async_copy(
                    source.at[c, pl.ds(start * PLANES, count * PLANES)],
                    cols.at[slab, pl.ds(0, count * PLANES)],
                    in_sem.at[slab],
                ))
        return copies

    for index in range(3):
        for copy in chunk_copies(index):
            copy.start()

    small_copies = [
        pltpu.make_async_copy(src, dst, in_sem.at[18 + k])
        for k, (src, dst) in enumerate(((stiff_hbm, stiff), (mass_hbm, mass), (table_hbm, table), (wrap_hbm, wrap)))
    ]
    for copy in small_copies:
        copy.start()

    barrier = pltpu.get_barrier_semaphore()
    def start(copies):
        first, last, make = copies

        @pl.loop(first, last)
        def _(k):
            make(k).start()

        return copies

    def arrive(copies):
        first, last, make = copies

        @pl.loop(first, last)
        def _(k):
            make(k).wait_recv()

    def leave(*groups):
        for first, last, make in groups:
            @pl.loop(first, last)
            def _(k, make=make):
                make(k).wait_send()

    def same_z(k):
        return zi * GROUP + lax.rem(i + k, GROUP)

    def along_z(k):
        return lax.rem(zi + k, GROUP) * GROUP + i

    @pl.loop(1, GROUP)
    def _(k):
        pl.semaphore_signal(barrier, inc=1, device_id=(s, same_z(k)), device_id_type=MESH)
        pl.semaphore_signal(barrier, inc=1, device_id=(s, along_z(k)), device_id_type=MESH)

    @pl.loop(1, SPAN)
    def _(k):
        pl.semaphore_signal(barrier, inc=1, device_id=(lax.rem(s + k, SPAN), d), device_id_type=MESH)

    def turned(b):
        return jnp.transpose(jnp.broadcast_to(bmap[pl.ds(b, 1), :], (ED, ED)))

    def hot_rows(b, here):
        following = turned(lax.rem(b + 1, NBE))
        lane = lax.broadcasted_iota(jnp.int32, (16, ED), 1)
        for r in range(0, ED, 16):
            tile = lax.shift_right_logical(here[r:r + 16], 7).astype(F32).astype(BF16)
            hot = jnp.where((here[r:r + 16] & (ED - 1)) == lane, 1.0, 0.0).astype(BF16)
            for j in range(TILES * TILE // ED):
                rows_hot[pl.ds(pl.multiple_of(b * ED + r, 16), 16), j * ED:(j + 1) * ED] = jnp.where(
                    tile == jnp.bfloat16(j), hot, jnp.zeros_like(hot)
                )
        return following

    lax.fori_loop(0, NBE, hot_rows, turned(0))

    for index in range(3):
        for copy in chunk_copies(index):
            copy.wait()

        @pl.loop(0, chunks[index][1])
        def _(q, index=index):
            here = pl.ds(pl.multiple_of(q * PLANES, PLANES), PLANES)

            def value(which, c):
                return cols[which * 9 + c * 3 + index, here].astype(F32)

            first = value(0, 0)
            advect = first * value(1, 0) + value(0, 1) * value(1, 1) + value(0, 2) * value(1, 2)
            row = pl.multiple_of((q + chunks[index][0]) * PLANES, PLANES)
            shifted[pl.ds(row, PLANES), :] = first - 0.5 * advect

    project_high, project_low = split(project[...])
    project_both = jnp.concatenate([project_high, project_low], axis=0)
    area = jnp.concatenate([jacobian[...], jacobian[...]], axis=1)
    loads = QP * PLANES

    @pl.loop(0, PLANES // 2, unroll=4)
    def _(pair):
        values = jnp.concatenate(
            [shifted[pl.ds(2 * pair + k, QP, stride=PLANES), :] for k in range(2)], axis=1
        )
        high, low = split(values)
        load = (both(dot(project_both, high)) + dot(project_high, low)) * area
        start = pl.multiple_of(loads + pair * 2 * NBE, 2 * NBE)
        shifted[pl.ds(start, NBE), :] = load[:, :ED]
        shifted[pl.ds(start + NBE, NBE), :] = load[:, ED:]

    @pl.loop(0, NBE, unroll=4)
    def _(b):
        high, low = split(shifted[pl.ds(loads + b, PLANES, stride=NBE), :])
        columns = pl.ds(pl.multiple_of(b * ED, ED), ED)
        parts[:PLANES, columns] = high
        parts[PLANES:, columns] = low

    def remote(inst, stage, k, src, dst, target):
        return pltpu.make_async_remote_copy(
            src_ref=src, dst_ref=dst, send_sem=dom_send.at[inst, stage, k], recv_sem=dom_recv.at[inst, stage, k],
            device_id=(s, target), device_id_type=MESH,
        )

    def across(stage, k, src, dst):
        return pltpu.make_async_remote_copy(
            src_ref=src, dst_ref=dst, send_sem=span_send.at[stage, k], recv_sem=span_recv.at[stage, k],
            device_id=(lax.rem(s + k, SPAN), d), device_id_type=MESH,
        )

    def rows_of(index):
        return pl.ds(pl.multiple_of(index * 8, 8), 8)

    def scatter_copies(inst):
        def make(k):
            peer = lax.rem(i + k, GROUP)
            return remote(inst, 0, k, msg.at[inst, rows_of(peer)], recv_a.at[inst, k], zi * GROUP + peer)

        return 1, GROUP, make

    def depth_copies(inst):
        own = recv_b.at[inst, zi]
        return 1, GROUP, lambda k: remote(inst, 1, k, own, own, along_z(k))

    def share_copies(inst):
        own = full.at[inst, rows_of(i)]
        return 1, GROUP, lambda k: remote(inst, 2, k, own, own, same_z(k))

    def scatter_sum(inst):
        return start(scatter_copies(inst))

    def depth_sum(inst):
        total = msg[inst, rows_of(i)]
        for k in range(1, GROUP):
            total = total + recv_a[inst, k]
        recv_b[inst, zi] = total
        return start(depth_copies(inst))

    def depth_total(inst):
        total = recv_b[inst, 0]
        for k in range(1, GROUP):
            total = total + recv_b[inst, k]
        return total

    def within(inst, stage, own):
        return start((1, GROUP, lambda k: remote(inst, stage, k, own, own, same_z(k))))

    def assemble(first, count):
        return both(dot(parts[...], rows_hot[:, first * TILE:(first + count) * TILE]))

    msg[0] = assemble(TILES - 1, 1)
    pl.semaphore_wait(barrier, 2 * (GROUP - 1) + SPAN - 1)
    int_a = scatter_sum(0)
    rows = pl.ds(pl.multiple_of(s * PLANES, PLANES), PLANES)

    def out_copy(k):
        return across(0, k, w8.at[pl.ds(2 * lax.rem(s + k, SPAN), 2)], cross.at[:, rows])

    @pl.loop(1, SPAN + 1)
    def _(k):
        j = lax.rem(s + k, SPAN)
        chunk = both(dot(parts[...], rows_hot[:, pl.ds(pl.multiple_of(j * 2 * TILE, 2 * TILE), 2 * TILE)]))
        for half in range(2):
            w8[2 * j + half] = chunk[:, half * TILE:(half + 1) * TILE]

        @pl.when(k < SPAN)
        def _():
            out_copy(k).start()

    out_copies = (1, SPAN, out_copy)
    cross[:, rows, :] = w8[pl.ds(2 * s, 2)]
    arrive(int_a)
    int_b = depth_sum(0)

    for copy in small_copies:
        copy.wait()
    wave = (lax.broadcasted_iota(jnp.int32, (PLANES // 2, ED), 0) + s * (PLANES // 2)).astype(F32) * (1.0 / SIZE)
    shift = 0.5 + 8.0 * wave * wave

    @pl.loop(0, NBE)
    def _(c):
        for b in range(NBE):
            row = pl.multiple_of((c * NBE + b) * (PLANES // 2), PLANES // 2)
            shifted[pl.ds(row, PLANES // 2), :] = stiff[c, pl.ds(b, 1), :] + shift * mass[c, pl.ds(b, 1), :]

    arrive(out_copies)

    @pl.loop(0, 2)
    def _(half):
        high, low = split(cross[half])
        modes[half] = both(dot(table[...], high)) + dot(table[:SIZE, :], low)

    def back_copy(k):
        there = pl.ds(pl.multiple_of(lax.rem(s + k, SPAN) * PLANES, PLANES), PLANES)
        return across(1, k, modes.at[:, there], r8.at[pl.ds(2 * s, 2)])

    back_copies = start((1, SPAN, back_copy))
    r8[pl.ds(2 * s, 2)] = modes[:, pl.ds(pl.multiple_of(s * PLANES, PLANES), PLANES), :]

    arrive(int_b)
    interface[i, s] = depth_total(0)
    int_c = start((1, SPAN, lambda k: across(2, k, interface.at[i, s], interface.at[i, s])))

    @pl.loop(0, NBE)
    def _(b):
        here = jnp.broadcast_to(bmap[pl.ds(b, 1), :], (16, ED))
        row = lax.broadcasted_iota(jnp.int32, (16, ED), 0)
        tile = lax.shift_right_logical(here, 4).astype(F32).astype(BF16)
        hot = jnp.where((here & 15) == row, 1.0, 0.0).astype(BF16)
        for g in range(TILES * TILE // 16):
            cols[b, pl.ds(g * 16, 16), :] = jnp.where(tile == jnp.bfloat16(g), hot, jnp.zeros_like(hot))

    arrive(int_c)
    int_d = within(0, 2, interface.at[i])
    for field in (a8, p8, x8, gathered_a, gathered_r):
        field[...] = jnp.zeros_like(field)

    def keep_parts(tile, values):
        high, low = split(values)
        columns = pl.ds(pl.multiple_of(tile * TILE, TILE), TILE)
        vparts[:PLANES, columns] = high
        vparts[PLANES:, columns] = low

    def gather_private(target):
        @pl.loop(0, 4)
        def _(n):
            hot = jnp.concatenate([cols[n * 8 + k, :PRIV] for k in range(8)], axis=1)
            out = both(dot(vparts[:, :PRIV], hot))
            for k in range(8):
                target[8 * n + k] = out[:, k * ED:(k + 1) * ED]

    def gather_interface(add, values):
        high, low = split(values)
        rest = (values - high.astype(F32) - low.astype(F32)).astype(BF16)
        lhs = jnp.concatenate([high, low, rest], axis=0)
        for n in range(4):
            hot = jnp.concatenate([cols[n * 8 + k, PRIV:] for k in range(8)], axis=1)
            out = dot(lhs, hot)
            out = out[:PLANES] + out[PLANES:2 * PLANES] + out[2 * PLANES:]
            for k in range(8):
                add(8 * n + k, out[:, k * ED:(k + 1) * ED])

    leave(out_copies)

    @pl.loop(0, SPAN)
    def _(turn):
        k = turn + turn // 2 - 2 * (turn // 3)
        j = lax.rem(s + SPAN - k, SPAN)

        @pl.when(turn > 0)
        def _():
            back_copy(k).wait_recv()

        for half in range(2):
            keep_parts(2 * j + half, jnp.where(2 * j + half < TILES - 1, r8[2 * j + half], 0.0))
        chunk = pl.ds(pl.multiple_of(j * 2 * TILE, 2 * TILE), 2 * TILE)

        @pl.loop(0, 4)
        def _(n):
            hot = jnp.concatenate([cols[n * 8 + m, chunk] for m in range(8)], axis=1)
            out = both(dot(vparts[:, chunk], hot))
            for m in range(8):
                gathered_r[8 * n + m] += out[:, m * ED:(m + 1) * ED]

    arrive(int_d)
    high, low = split(interface[...].reshape(SIZE, TILE))
    wrap_high = wrap[pl.ds(pl.multiple_of(s * PLANES, PLANES), PLANES), :]
    wrap_low = wrap[pl.ds(pl.multiple_of(SIZE + s * PLANES, PLANES), PLANES), :]
    r_int = dot(wrap_high, high) + dot(wrap_low, high) + dot(wrap_high, low)
    r8[TILES - 1] = r_int

    def add_first(b, values):
        gathered_r[b] += values

    gather_interface(add_first, r_int)
    leave(int_a, int_b, int_c, int_d, back_copies)

    def assemble_private():
        @pl.loop(0, TILES // 2)
        def _(pair):
            columns = pl.ds(pl.multiple_of(pair * 2 * TILE, 2 * TILE), 2 * TILE)
            out = both(dot(parts[...], rows_hot[:, columns]))
            for half in range(2):
                values = out[:, half * TILE:(half + 1) * TILE]
                w8[2 * pair + half] = values
                keep_parts(2 * pair + half, values)

    lane = lax.broadcasted_iota(jnp.int32, (PLANES, ED), 1)
    extra = jnp.where(s == 0, 2.0, 0.0)
    top = lax.broadcasted_iota(jnp.int32, (PLANES // 2, ED), 0) == 0
    half_rows = PLANES // 2
    block = 4

    def operate(source):
        special = source[:, half_rows, :] * extra

        @pl.loop(0, NBE // block)
        def _(step):
            sums = [[jnp.zeros((half_rows, ED), F32) for _ in range(2)] for _ in range(block)]
            for b in range(NBE):
                even = source[b, :half_rows]
                odd = source[b, half_rows:]
                for k in range(block):
                    row = pl.multiple_of(((step * block + k) * NBE + b) * half_rows, half_rows)
                    matrix = shifted[pl.ds(row, half_rows), :]
                    sums[k][0] = sums[k][0] + matrix * even
                    sums[k][1] = sums[k][1] + matrix * odd
            for k in range(block):
                gathered_w[step * block + k, :half_rows] = sums[k][0]
                gathered_w[step * block + k, half_rows:] = sums[k][1]

        def column(c, products):
            fix = jnp.sum(mass[c] * special, axis=0, keepdims=True)
            image = jnp.concatenate(
                [gathered_w[c, :half_rows], gathered_w[c, half_rows:] + jnp.where(top, fix, 0.0)], axis=0
            )
            high, low = split(image)
            columns = pl.ds(pl.multiple_of(c * ED, ED), ED)
            parts[:PLANES, columns] = high
            parts[PLANES:, columns] = low
            return products + image * source[c]

        products = lax.fori_loop(0, NBE, column, jnp.zeros((PLANES, ED), F32), unroll=4)
        return jnp.sum(products, axis=1, keepdims=True)

    def product_sum(left, right):
        total = left[0] * right[0]
        for t in range(1, TILES - 1):
            total = total + left[t] * right[t]
        return jnp.sum(total, axis=1, keepdims=True)

    state[0] = jnp.ones((PLANES, ED), F32)
    state[1] = jnp.zeros((PLANES, ED), F32)

    @pl.loop(0, 3)
    def _(step):
        rw = operate(gathered_r)
        rr = product_sum(r8, r8)
        ra = product_sum(r8, a8)
        own = jnp.where(lane == 0, rr, jnp.where(lane == 1, rw, jnp.where(lane == 2, ra, 0.0)))

        inst = step + 1
        dots_a[step, i] = jnp.transpose(jnp.concatenate([own, jnp.zeros_like(own)], axis=0))[:8]
        dots_first = within(inst, 3, dots_a.at[step, i])

        @pl.when(step < 2)
        def _():
            msg[inst] = assemble(TILES - 1, 1)
            scatter_sum(inst)
            assemble_private()

        arrive(dots_first)
        total = dots_a[step, 0]
        for k in range(1, GROUP):
            total = total + dots_a[step, k]
        dots_b[step, zi] = total
        dots_second = start((1, GROUP, lambda k: remote(
            inst, 4, k, dots_b.at[step, zi], dots_b.at[step, zi], along_z(k)
        )))

        @pl.when(step < 2)
        def _():
            arrive(scatter_copies(inst))
            depth_sum(inst)
            gather_private(gathered_w)
            arrive(depth_copies(inst))
            full[inst, rows_of(i)] = depth_total(inst)
            start(share_copies(inst))

        arrive(dots_second)
        total = dots_b[step, 0]
        for k in range(1, GROUP):
            total = total + dots_b[step, k]
        dots = jnp.transpose(jnp.concatenate([total, jnp.zeros((ED - 8, ED), F32)], axis=0))[:PLANES]
        r_int = r8[TILES - 1]
        rr = dots[:, 0:1] + jnp.sum(r_int * r_int, axis=1, keepdims=True)
        rw = dots[:, 1:2]
        ra = dots[:, 2:3] + jnp.sum(r_int * a8[TILES - 1], axis=1, keepdims=True)
        beta = jnp.where(step == 0, 0.0, rr / state[0, :, 0:1])
        energy = rw + 2.0 * beta * ra + beta * beta * state[1, :, 0:1]
        state[0] = jnp.broadcast_to(rr, (PLANES, ED))
        state[1] = jnp.broadcast_to(energy, (PLANES, ED))
        factors[0] = jnp.broadcast_to(rr / energy, (PLANES, TILE))
        factors[1] = jnp.broadcast_to(beta, (PLANES, TILE))

        def advance(t, values):
            image = values + factors[1] * a8[t]
            a8[t] = image
            r8[t] = r8[t] - factors[0] * image

        @pl.loop(0, TILES)
        def _(t):
            direction = r8[t] + factors[1] * p8[t]
            p8[t] = direction
            x8[t] = x8[t] + factors[0] * direction

        @pl.when(step < 2)
        def _():
            @pl.loop(0, TILES - 1)
            def _(t):
                advance(t, w8[t])

            @pl.loop(0, NBE, unroll=2)
            def _(b):
                image = gathered_w[b] + factors[1, :, :ED] * gathered_a[b]
                gathered_a[b] = image
                gathered_r[b] = gathered_r[b] - factors[0, :, :ED] * image

            arrive(share_copies(inst))
            advance(TILES - 1, full[inst])

            def add(b, values):
                gathered_a[b] += values
                gathered_r[b] = gathered_r[b] - factors[0, :, :ED] * values

            gather_interface(add, full[inst])
            leave(scatter_copies(inst), depth_copies(inst), share_copies(inst))

        leave(dots_first, dots_second)

    @pl.loop(0, TILES)
    def _(t):
        for part in range(2):
            slab = out.at[2 * t + part]
            for parity in range(2):
                mine = x8[t, parity * half_rows:(parity + 1) * half_rows, part * ED:(part + 1) * ED]
                slab[pl.ds(parity, half_rows, stride=2), :] = mine


def place(slabs, out_private, out_interface):
    for n in range(TILES * TILE // ED):
        if n < PRIV // ED:
            out_private[:, n * ED:(n + 1) * ED] = slabs[n]
        else:
            out_interface[:, n * ED - PRIV:(n + 1) * ED - PRIV] = slabs[n]


def shards(velocity, gradient, project_table, jacobian, stiff_elem, mass_elem, bound_map):
    order = np.arange(SIZE).reshape(SPAN, PLANES // 2, 2).transpose(0, 2, 1).reshape(-1)
    table = spanwise_table()[order]
    wrap = table[:, np.arange(SIZE).reshape(SPAN, GROUP, 8).transpose(1, 0, 2).reshape(-1)]

    def in_parts(values):
        high = values.astype(BF16)
        return jnp.asarray(np.concatenate([high, (values - high.astype(np.float32)).astype(BF16)], axis=0))

    vmem = pl.BlockSpec(memory_space=pltpu.VMEM)
    hbm = pl.BlockSpec(memory_space=pl.ANY)
    field = pltpu.VMEM((TILES, PLANES, TILE), F32)
    spread = pltpu.VMEM((NBE, PLANES, ED), F32)
    slabs = pl.pallas_call(
        kernel,
        out_shape=jax.ShapeDtypeStruct((TILES * TILE // ED, PLANES, ED), F32),
        in_specs=[hbm, hbm] + [vmem] * 3 + [hbm] * 4,
        out_specs=vmem,
        scratch_shapes=[
            pltpu.VMEM((NBE, NBE, ED), F32),
            pltpu.VMEM((NBE, NBE, ED), F32),
            pltpu.VMEM((2 * SIZE, SIZE), BF16),
            pltpu.VMEM((2 * SIZE, SIZE), BF16),
            pltpu.VMEM((NBE, TILES * TILE, ED), BF16),
            pltpu.VMEM((NBE * ED, TILES * TILE), BF16),
            pltpu.VMEM((NBE * NBE * PLANES // 2, ED), F32),
            pltpu.VMEM((2 * PLANES, NBE * ED), BF16),
            pltpu.VMEM((2 * PLANES, TILES * TILE), BF16),
            spread, spread, spread,
            field, field, field, field, field,
            pltpu.VMEM((2, SIZE, TILE), F32),
            pltpu.VMEM((2, SIZE, TILE), F32),
            pltpu.VMEM((GROUP, SPAN, 8, TILE), F32),
            pltpu.VMEM((3, PLANES, TILE), F32),
            pltpu.VMEM((3, GROUP, 8, TILE), F32),
            pltpu.VMEM((3, GROUP, 8, TILE), F32),
            pltpu.VMEM((3, PLANES, TILE), F32),
            pltpu.VMEM((3, GROUP, 8, ED), F32),
            pltpu.VMEM((3, GROUP, 8, ED), F32),
            pltpu.VMEM((2, PLANES, TILE), F32),
            pltpu.VMEM((2, PLANES, ED), F32),
            pltpu.SemaphoreType.DMA((22,)),
            pltpu.SemaphoreType.DMA((3, SPAN)),
            pltpu.SemaphoreType.DMA((3, SPAN)),
            pltpu.SemaphoreType.DMA((4, 5, GROUP)),
            pltpu.SemaphoreType.DMA((4, 5, GROUP)),
        ],
        compiler_params=pltpu.CompilerParams(
            collective_id=0, has_side_effects=True, vmem_limit_bytes=62 * 1024 * 1024
        ),
    )(
        jnp.transpose(velocity, (0, 2, 1, 3)).reshape(3, QP * PLANES, ED),
        jnp.transpose(gradient, (0, 2, 1, 3)).reshape(3, QP * PLANES, ED),
        project_table.T,
        jacobian.reshape(1, ED),
        bound_map,
        stiff_elem,
        mass_elem,
        in_parts(table),
        in_parts(wrap),
    )
    return pl.pallas_call(
        place,
        out_shape=(jax.ShapeDtypeStruct((PLANES, PRIV), F32), jax.ShapeDtypeStruct((PLANES, TILE), F32)),
        in_specs=[vmem],
        out_specs=(vmem, vmem),
    )(slabs)


def solution(mesh):
    return jax.shard_map(
        shards,
        mesh=mesh,
        in_specs=(
            P(None, "span", None, "dom"),
            P(None, "span", None, "dom"),
            P(),
            P("dom"),
            P(None, None, "dom"),
            P(None, None, "dom"),
            P(None, "dom"),
        ),
        out_specs=(P("span", "dom"), P("span", None)),
        check_vma=False,
    )
```

```python
import jax
import jax.numpy as jnp
import numpy as np
from jax import lax
from jax.experimental import pallas as pl
from jax.experimental.pallas import tpu as pltpu
from jax.sharding import PartitionSpec as P

MESH = pl.DeviceIdType.MESH
F32 = jnp.float32
BF16 = jnp.bfloat16
QP = 81
NBE = 32
ED = 128
PLANES = 64
SIZE = 256
SPAN = 4
TILES = 8
TILE = 256
PRIV = 1792
GROUP = 8


def spanwise_table():
    index = np.arange(SIZE)
    kappa = np.where(index == 1, SIZE // 2, index // 2)
    angle = 2.0 * np.pi / SIZE * ((kappa[:, None] * index[None, :]) % SIZE)
    scale = np.where(index < 2, np.sqrt(1.0 / SIZE), np.sqrt(2.0 / SIZE))
    odd = (index % 2 == 1) & (index != 1)
    return (np.where(odd[:, None], -np.sin(angle), np.cos(angle)) * scale[:, None]).astype(np.float32)


def split(values):
    high = values.astype(BF16)
    return high, (values - high.astype(F32)).astype(BF16)


def both(product):
    half = product.shape[0] // 2
    return product[:half] + product[half:]


def dot(left, right):
    return jnp.dot(left, right, preferred_element_type=F32)


def kernel(
    vel_hbm, grad_hbm, project, jacobian, bmap, stiff_hbm, mass_hbm, table_hbm, wrap_hbm,
    out,
    stiff, mass, table, wrap, cols, rows_hot, shifted, parts, vparts, gathered_w, gathered_a, gathered_r,
    w8, a8, p8, r8, x8, cross, modes, interface,
    msg, recv_a, recv_b, full, dots_a, dots_b, factors, state,
    in_sem, span_send, span_recv, dom_send, dom_recv,
):
    s = lax.axis_index("span")
    d = lax.axis_index("dom")
    zi = lax.div(d, GROUP)
    i = lax.rem(d, GROUP)

    chunks = [(0, 32), (32, 32), (64, QP - 64)]

    def chunk_copies(index):
        start, count = chunks[index]
        copies = []
        for which, source in enumerate((vel_hbm, grad_hbm)):
            for c in range(3):
                slab = which * 9 + c * 3 + index
                copies.append(pltpu.make_async_copy(
                    source.at[c, pl.ds(start * PLANES, count * PLANES)],
                    cols.at[slab, pl.ds(0, count * PLANES)],
                    in_sem.at[slab],
                ))
        return copies

    for index in range(3):
        for copy in chunk_copies(index):
            copy.start()

    small_copies = [
        pltpu.make_async_copy(src, dst, in_sem.at[18 + k])
        for k, (src, dst) in enumerate(((stiff_hbm, stiff), (mass_hbm, mass), (table_hbm, table), (wrap_hbm, wrap)))
    ]
    for copy in small_copies:
        copy.start()

    barrier = pltpu.get_barrier_semaphore()
    def start(copies):
        first, last, make = copies

        @pl.loop(first, last)
        def _(k):
            make(k).start()

        return copies

    def arrive(copies):
        first, last, make = copies

        @pl.loop(first, last)
        def _(k):
            make(k).wait_recv()

    def leave(*groups):
        for first, last, make in groups:
            @pl.loop(first, last)
            def _(k, make=make):
                make(k).wait_send()

    def same_z(k):
        return zi * GROUP + lax.rem(i + k, GROUP)

    def along_z(k):
        return lax.rem(zi + k, GROUP) * GROUP + i

    @pl.loop(1, GROUP)
    def _(k):
        pl.semaphore_signal(barrier, inc=1, device_id=(s, same_z(k)), device_id_type=MESH)
        pl.semaphore_signal(barrier, inc=1, device_id=(s, along_z(k)), device_id_type=MESH)

    @pl.loop(1, SPAN)
    def _(k):
        pl.semaphore_signal(barrier, inc=1, device_id=(lax.rem(s + k, SPAN), d), device_id_type=MESH)

    def turned(b):
        return jnp.transpose(jnp.broadcast_to(bmap[pl.ds(b, 1), :], (ED, ED)))

    def hot_rows(b, here):
        following = turned(lax.rem(b + 1, NBE))
        lane = lax.broadcasted_iota(jnp.int32, (16, ED), 1)
        for r in range(0, ED, 16):
            tile = lax.shift_right_logical(here[r:r + 16], 7).astype(F32).astype(BF16)
            hot = jnp.where((here[r:r + 16] & (ED - 1)) == lane, 1.0, 0.0).astype(BF16)
            for j in range(TILES * TILE // ED):
                rows_hot[pl.ds(pl.multiple_of(b * ED + r, 16), 16), j * ED:(j + 1) * ED] = jnp.where(
                    tile == jnp.bfloat16(j), hot, jnp.zeros_like(hot)
                )
        return following

    lax.fori_loop(0, NBE, hot_rows, turned(0))

    for index in range(3):
        for copy in chunk_copies(index):
            copy.wait()

        @pl.loop(0, chunks[index][1])
        def _(q, index=index):
            here = pl.ds(pl.multiple_of(q * PLANES, PLANES), PLANES)

            def value(which, c):
                return cols[which * 9 + c * 3 + index, here].astype(F32)

            first = value(0, 0)
            advect = first * value(1, 0) + value(0, 1) * value(1, 1) + value(0, 2) * value(1, 2)
            row = pl.multiple_of((q + chunks[index][0]) * PLANES, PLANES)
            shifted[pl.ds(row, PLANES), :] = first - 0.5 * advect

    project_high, project_low = split(project[...])
    project_both = jnp.concatenate([project_high, project_low], axis=0)
    area = jnp.concatenate([jacobian[...], jacobian[...]], axis=1)
    loads = QP * PLANES

    @pl.loop(0, PLANES // 2, unroll=4)
    def _(pair):
        values = jnp.concatenate(
            [shifted[pl.ds(2 * pair + k, QP, stride=PLANES), :] for k in range(2)], axis=1
        )
        high, low = split(values)
        load = (both(dot(project_both, high)) + dot(project_high, low)) * area
        start = pl.multiple_of(loads + pair * 2 * NBE, 2 * NBE)
        shifted[pl.ds(start, NBE), :] = load[:, :ED]
        shifted[pl.ds(start + NBE, NBE), :] = load[:, ED:]

    @pl.loop(0, NBE, unroll=4)
    def _(b):
        high, low = split(shifted[pl.ds(loads + b, PLANES, stride=NBE), :])
        columns = pl.ds(pl.multiple_of(b * ED, ED), ED)
        parts[:PLANES, columns] = high
        parts[PLANES:, columns] = low

    def remote(inst, stage, k, src, dst, target):
        return pltpu.make_async_remote_copy(
            src_ref=src, dst_ref=dst, send_sem=dom_send.at[inst, stage, k], recv_sem=dom_recv.at[inst, stage, k],
            device_id=(s, target), device_id_type=MESH,
        )

    def across(stage, k, src, dst):
        return pltpu.make_async_remote_copy(
            src_ref=src, dst_ref=dst, send_sem=span_send.at[stage, k], recv_sem=span_recv.at[stage, k],
            device_id=(lax.rem(s + k, SPAN), d), device_id_type=MESH,
        )

    def rows_of(index):
        return pl.ds(pl.multiple_of(index * 8, 8), 8)

    def scatter_copies(inst):
        def make(k):
            peer = lax.rem(i + k, GROUP)
            return remote(inst, 0, k, msg.at[inst, rows_of(peer)], recv_a.at[inst, k], zi * GROUP + peer)

        return 1, GROUP, make

    def depth_copies(inst):
        own = recv_b.at[inst, zi]
        return 1, GROUP, lambda k: remote(inst, 1, k, own, own, along_z(k))

    def share_copies(inst):
        own = full.at[inst, rows_of(i)]
        return 1, GROUP, lambda k: remote(inst, 2, k, own, own, same_z(k))

    def scatter_sum(inst):
        return start(scatter_copies(inst))

    def depth_sum(inst):
        total = msg[inst, rows_of(i)]
        for k in range(1, GROUP):
            total = total + recv_a[inst, k]
        recv_b[inst, zi] = total
        return start(depth_copies(inst))

    def depth_total(inst):
        total = recv_b[inst, 0]
        for k in range(1, GROUP):
            total = total + recv_b[inst, k]
        return total

    def within(inst, stage, own):
        return start((1, GROUP, lambda k: remote(inst, stage, k, own, own, same_z(k))))

    def assemble(first, count):
        return both(dot(parts[...], rows_hot[:, first * TILE:(first + count) * TILE]))

    msg[0] = assemble(TILES - 1, 1)
    pl.semaphore_wait(barrier, 2 * (GROUP - 1) + SPAN - 1)
    int_a = scatter_sum(0)
    rows = pl.ds(pl.multiple_of(s * PLANES, PLANES), PLANES)

    def out_copy(k):
        return across(0, k, w8.at[pl.ds(2 * lax.rem(s + k, SPAN), 2)], cross.at[:, rows])

    @pl.loop(1, SPAN + 1)
    def _(turn):
        k = turn + jnp.where(turn == 1, 1, jnp.where(turn == 2, -1, 0))
        j = lax.rem(s + k, SPAN)
        chunk = both(dot(parts[...], rows_hot[:, pl.ds(pl.multiple_of(j * 2 * TILE, 2 * TILE), 2 * TILE)]))
        for half in range(2):
            w8[2 * j + half] = chunk[:, half * TILE:(half + 1) * TILE]

        @pl.when(k < SPAN)
        def _():
            out_copy(k).start()

    out_copies = (1, SPAN, out_copy)
    cross[:, rows, :] = w8[pl.ds(2 * s, 2)]
    arrive(int_a)
    int_b = depth_sum(0)

    for copy in small_copies:
        copy.wait()
    wave = (lax.broadcasted_iota(jnp.int32, (PLANES // 2, ED), 0) + s * (PLANES // 2)).astype(F32) * (1.0 / SIZE)
    shift = 0.5 + 8.0 * wave * wave

    @pl.loop(0, NBE)
    def _(c):
        for b in range(NBE):
            row = pl.multiple_of((c * NBE + b) * (PLANES // 2), PLANES // 2)
            shifted[pl.ds(row, PLANES // 2), :] = stiff[c, pl.ds(b, 1), :] + shift * mass[c, pl.ds(b, 1), :]

    arrive(out_copies)

    @pl.loop(0, 2)
    def _(half):
        high, low = split(cross[half])
        modes[half] = both(dot(table[...], high)) + dot(table[:SIZE, :], low)

    def back_copy(k):
        there = pl.ds(pl.multiple_of(lax.rem(s + k, SPAN) * PLANES, PLANES), PLANES)
        return across(1, k, modes.at[:, there], r8.at[pl.ds(2 * s, 2)])

    back_copies = start((1, SPAN, back_copy))
    r8[pl.ds(2 * s, 2)] = modes[:, pl.ds(pl.multiple_of(s * PLANES, PLANES), PLANES), :]

    arrive(int_b)
    interface[i, s] = depth_total(0)
    int_c = start((1, SPAN, lambda k: across(2, k, interface.at[i, s], interface.at[i, s])))

    @pl.loop(0, NBE)
    def _(b):
        here = jnp.broadcast_to(bmap[pl.ds(b, 1), :], (16, ED))
        row = lax.broadcasted_iota(jnp.int32, (16, ED), 0)
        tile = lax.shift_right_logical(here, 4).astype(F32).astype(BF16)
        hot = jnp.where((here & 15) == row, 1.0, 0.0).astype(BF16)
        for g in range(TILES * TILE // 16):
            cols[b, pl.ds(g * 16, 16), :] = jnp.where(tile == jnp.bfloat16(g), hot, jnp.zeros_like(hot))

    arrive(int_c)
    int_d = within(0, 2, interface.at[i])
    for field in (a8, p8, x8, gathered_a, gathered_r):
        field[...] = jnp.zeros_like(field)

    def keep_parts(tile, values):
        high, low = split(values)
        columns = pl.ds(pl.multiple_of(tile * TILE, TILE), TILE)
        vparts[:PLANES, columns] = high
        vparts[PLANES:, columns] = low

    def gather_private(target):
        @pl.loop(0, 4)
        def _(n):
            hot = jnp.concatenate([cols[n * 8 + k, :PRIV] for k in range(8)], axis=1)
            out = both(dot(vparts[:, :PRIV], hot))
            for k in range(8):
                target[8 * n + k] = out[:, k * ED:(k + 1) * ED]

    def gather_interface(add, values):
        high, low = split(values)
        rest = (values - high.astype(F32) - low.astype(F32)).astype(BF16)
        lhs = jnp.concatenate([high, low, rest], axis=0)
        for n in range(4):
            hot = jnp.concatenate([cols[n * 8 + k, PRIV:] for k in range(8)], axis=1)
            out = dot(lhs, hot)
            out = out[:PLANES] + out[PLANES:2 * PLANES] + out[2 * PLANES:]
            for k in range(8):
                add(8 * n + k, out[:, k * ED:(k + 1) * ED])

    leave(out_copies)

    @pl.loop(0, SPAN)
    def _(turn):
        k = turn + turn // 2 - 2 * (turn // 3)
        j = lax.rem(s + SPAN - k, SPAN)

        @pl.when(turn > 0)
        def _():
            back_copy(k).wait_recv()

        for half in range(2):
            keep_parts(2 * j + half, jnp.where(2 * j + half < TILES - 1, r8[2 * j + half], 0.0))
        chunk = pl.ds(pl.multiple_of(j * 2 * TILE, 2 * TILE), 2 * TILE)

        @pl.loop(0, 4)
        def _(n):
            hot = jnp.concatenate([cols[n * 8 + m, chunk] for m in range(8)], axis=1)
            out = both(dot(vparts[:, chunk], hot))
            for m in range(8):
                gathered_r[8 * n + m] += out[:, m * ED:(m + 1) * ED]

    arrive(int_d)
    high, low = split(interface[...].reshape(SIZE, TILE))
    wrap_high = wrap[pl.ds(pl.multiple_of(s * PLANES, PLANES), PLANES), :]
    wrap_low = wrap[pl.ds(pl.multiple_of(SIZE + s * PLANES, PLANES), PLANES), :]
    r_int = dot(wrap_high, high) + dot(wrap_low, high) + dot(wrap_high, low)
    r8[TILES - 1] = r_int

    def add_first(b, values):
        gathered_r[b] += values

    gather_interface(add_first, r_int)
    leave(int_a, int_b, int_c, int_d, back_copies)

    def assemble_private():
        @pl.loop(0, TILES // 2)
        def _(pair):
            columns = pl.ds(pl.multiple_of(pair * 2 * TILE, 2 * TILE), 2 * TILE)
            out = both(dot(parts[...], rows_hot[:, columns]))
            for half in range(2):
                values = out[:, half * TILE:(half + 1) * TILE]
                w8[2 * pair + half] = values
                keep_parts(2 * pair + half, values)

    lane = lax.broadcasted_iota(jnp.int32, (PLANES, ED), 1)
    extra = jnp.where(s == 0, 2.0, 0.0)
    top = lax.broadcasted_iota(jnp.int32, (PLANES // 2, ED), 0) == 0
    half_rows = PLANES // 2
    block = 4

    def operate(source):
        special = source[:, half_rows, :] * extra

        @pl.loop(0, NBE // block)
        def _(step):
            sums = [[jnp.zeros((half_rows, ED), F32) for _ in range(2)] for _ in range(block)]
            for b in range(NBE):
                even = source[b, :half_rows]
                odd = source[b, half_rows:]
                for k in range(block):
                    row = pl.multiple_of(((step * block + k) * NBE + b) * half_rows, half_rows)
                    matrix = shifted[pl.ds(row, half_rows), :]
                    sums[k][0] = sums[k][0] + matrix * even
                    sums[k][1] = sums[k][1] + matrix * odd
            for k in range(block):
                gathered_w[step * block + k, :half_rows] = sums[k][0]
                gathered_w[step * block + k, half_rows:] = sums[k][1]

        def column(c, products):
            fix = jnp.sum(mass[c] * special, axis=0, keepdims=True)
            image = jnp.concatenate(
                [gathered_w[c, :half_rows], gathered_w[c, half_rows:] + jnp.where(top, fix, 0.0)], axis=0
            )
            high, low = split(image)
            columns = pl.ds(pl.multiple_of(c * ED, ED), ED)
            parts[:PLANES, columns] = high
            parts[PLANES:, columns] = low
            return products + image * source[c]

        products = lax.fori_loop(0, NBE, column, jnp.zeros((PLANES, ED), F32), unroll=4)
        return jnp.sum(products, axis=1, keepdims=True)

    def product_sum(left, right):
        total = left[0] * right[0]
        for t in range(1, TILES - 1):
            total = total + left[t] * right[t]
        return jnp.sum(total, axis=1, keepdims=True)

    def keep_dots():
        rr = product_sum(r8, r8)
        ra = product_sum(r8, a8)
        state[2] = jnp.where(lane == 0, rr, jnp.where(lane == 2, ra, 0.0))

    state[0] = jnp.ones((PLANES, ED), F32)
    state[1] = jnp.zeros((PLANES, ED), F32)

    keep_dots()

    @pl.loop(0, 3)
    def _(step):
        rw = operate(gathered_r)
        own = jnp.where(lane == 1, rw, state[2])

        inst = step + 1
        dots_a[step, i] = jnp.transpose(jnp.concatenate([own, jnp.zeros_like(own)], axis=0))[:8]
        dots_first = within(inst, 3, dots_a.at[step, i])

        @pl.when(step < 2)
        def _():
            msg[inst] = assemble(TILES - 1, 1)
            scatter_sum(inst)
            assemble_private()

        arrive(dots_first)
        total = dots_a[step, 0]
        for k in range(1, GROUP):
            total = total + dots_a[step, k]
        dots_b[step, zi] = total
        dots_second = start((1, GROUP, lambda k: remote(
            inst, 4, k, dots_b.at[step, zi], dots_b.at[step, zi], along_z(k)
        )))

        @pl.when(step < 2)
        def _():
            arrive(scatter_copies(inst))
            depth_sum(inst)
            gather_private(gathered_w)
            arrive(depth_copies(inst))
            full[inst, rows_of(i)] = depth_total(inst)
            start(share_copies(inst))

        arrive(dots_second)
        total = dots_b[step, 0]
        for k in range(1, GROUP):
            total = total + dots_b[step, k]
        dots = jnp.transpose(jnp.concatenate([total, jnp.zeros((ED - 8, ED), F32)], axis=0))[:PLANES]
        r_int = r8[TILES - 1]
        rr = dots[:, 0:1] + jnp.sum(r_int * r_int, axis=1, keepdims=True)
        rw = dots[:, 1:2]
        ra = dots[:, 2:3] + jnp.sum(r_int * a8[TILES - 1], axis=1, keepdims=True)
        beta = jnp.where(step == 0, 0.0, rr / state[0, :, 0:1])
        energy = rw + 2.0 * beta * ra + beta * beta * state[1, :, 0:1]
        state[0] = jnp.broadcast_to(rr, (PLANES, ED))
        state[1] = jnp.broadcast_to(energy, (PLANES, ED))
        factors[0] = jnp.broadcast_to(rr / energy, (PLANES, TILE))
        factors[1] = jnp.broadcast_to(beta, (PLANES, TILE))

        def advance(t, values):
            image = values + factors[1] * a8[t]
            a8[t] = image
            r8[t] = r8[t] - factors[0] * image

        @pl.loop(0, TILES)
        def _(t):
            direction = r8[t] + factors[1] * p8[t]
            p8[t] = direction
            x8[t] = x8[t] + factors[0] * direction

        @pl.when(step < 2)
        def _():
            @pl.loop(0, TILES - 1)
            def _(t):
                advance(t, w8[t])

            @pl.loop(0, NBE, unroll=2)
            def _(b):
                image = gathered_w[b] + factors[1, :, :ED] * gathered_a[b]
                gathered_a[b] = image
                gathered_r[b] = gathered_r[b] - factors[0, :, :ED] * image

            keep_dots()
            arrive(share_copies(inst))
            advance(TILES - 1, full[inst])

            def add(b, values):
                gathered_a[b] += values
                gathered_r[b] = gathered_r[b] - factors[0, :, :ED] * values

            gather_interface(add, full[inst])
            leave(scatter_copies(inst), depth_copies(inst), share_copies(inst))

        leave(dots_first, dots_second)

    @pl.loop(0, TILES)
    def _(t):
        for part in range(2):
            slab = out.at[2 * t + part]
            for parity in range(2):
                mine = x8[t, parity * half_rows:(parity + 1) * half_rows, part * ED:(part + 1) * ED]
                slab[pl.ds(parity, half_rows, stride=2), :] = mine


def place(slabs, out_private, out_interface):
    for n in range(TILES * TILE // ED):
        if n < PRIV // ED:
            out_private[:, n * ED:(n + 1) * ED] = slabs[n]
        else:
            out_interface[:, n * ED - PRIV:(n + 1) * ED - PRIV] = slabs[n]


def shards(velocity, gradient, project_table, jacobian, stiff_elem, mass_elem, bound_map):
    order = np.arange(SIZE).reshape(SPAN, PLANES // 2, 2).transpose(0, 2, 1).reshape(-1)
    table = spanwise_table()[order]
    wrap = table[:, np.arange(SIZE).reshape(SPAN, GROUP, 8).transpose(1, 0, 2).reshape(-1)]

    def in_parts(values):
        high = values.astype(BF16)
        return jnp.asarray(np.concatenate([high, (values - high.astype(np.float32)).astype(BF16)], axis=0))

    vmem = pl.BlockSpec(memory_space=pltpu.VMEM)
    hbm = pl.BlockSpec(memory_space=pl.ANY)
    field = pltpu.VMEM((TILES, PLANES, TILE), F32)
    spread = pltpu.VMEM((NBE, PLANES, ED), F32)
    slabs = pl.pallas_call(
        kernel,
        out_shape=jax.ShapeDtypeStruct((TILES * TILE // ED, PLANES, ED), F32),
        in_specs=[hbm, hbm] + [vmem] * 3 + [hbm] * 4,
        out_specs=vmem,
        scratch_shapes=[
            pltpu.VMEM((NBE, NBE, ED), F32),
            pltpu.VMEM((NBE, NBE, ED), F32),
            pltpu.VMEM((2 * SIZE, SIZE), BF16),
            pltpu.VMEM((2 * SIZE, SIZE), BF16),
            pltpu.VMEM((NBE, TILES * TILE, ED), BF16),
            pltpu.VMEM((NBE * ED, TILES * TILE), BF16),
            pltpu.VMEM((NBE * NBE * PLANES // 2, ED), F32),
            pltpu.VMEM((2 * PLANES, NBE * ED), BF16),
            pltpu.VMEM((2 * PLANES, TILES * TILE), BF16),
            spread, spread, spread,
            field, field, field, field, field,
            pltpu.VMEM((2, SIZE, TILE), F32),
            pltpu.VMEM((2, SIZE, TILE), F32),
            pltpu.VMEM((GROUP, SPAN, 8, TILE), F32),
            pltpu.VMEM((3, PLANES, TILE), F32),
            pltpu.VMEM((3, GROUP, 8, TILE), F32),
            pltpu.VMEM((3, GROUP, 8, TILE), F32),
            pltpu.VMEM((3, PLANES, TILE), F32),
            pltpu.VMEM((3, GROUP, 8, ED), F32),
            pltpu.VMEM((3, GROUP, 8, ED), F32),
            pltpu.VMEM((2, PLANES, TILE), F32),
            pltpu.VMEM((3, PLANES, ED), F32),
            pltpu.SemaphoreType.DMA((22,)),
            pltpu.SemaphoreType.DMA((3, SPAN)),
            pltpu.SemaphoreType.DMA((3, SPAN)),
            pltpu.SemaphoreType.DMA((4, 5, GROUP)),
            pltpu.SemaphoreType.DMA((4, 5, GROUP)),
        ],
        compiler_params=pltpu.CompilerParams(
            collective_id=0, has_side_effects=True, vmem_limit_bytes=62 * 1024 * 1024
        ),
    )(
        jnp.transpose(velocity, (0, 2, 1, 3)).reshape(3, QP * PLANES, ED),
        jnp.transpose(gradient, (0, 2, 1, 3)).reshape(3, QP * PLANES, ED),
        project_table.T,
        jacobian.reshape(1, ED),
        bound_map,
        stiff_elem,
        mass_elem,
        in_parts(table),
        in_parts(wrap),
    )
    return pl.pallas_call(
        place,
        out_shape=(jax.ShapeDtypeStruct((PLANES, PRIV), F32), jax.ShapeDtypeStruct((PLANES, TILE), F32)),
        in_specs=[vmem],
        out_specs=(vmem, vmem),
    )(slabs)


def solution(mesh):
    return jax.shard_map(
        shards,
        mesh=mesh,
        in_specs=(
            P(None, "span", None, "dom"),
            P(None, "span", None, "dom"),
            P(),
            P("dom"),
            P(None, None, "dom"),
            P(None, None, "dom"),
            P(None, "dom"),
        ),
        out_specs=(P("span", "dom"), P("span", None)),
        check_vma=False,
    )
```
